768 devices in a mesh: row: 16 (over y_lo, x, core), col: 48 (over y_hi, z).
Axes of the slice: x: 4, y: 8 (y_hi: 4, y_lo: 2; y = y_hi * 2 + y_lo), z: 12, core: 2. Of those that a mesh axis runs over, the one named last changes fastest.
Arguments:
- features: bfloat16 [98304, 128], P(('col', 'row')), may hold values from -6 to 6
- weight: bfloat16 [128, 256], replicated, may hold values from -0.5 to 0.5
- out_bias: float32 [256], replicated, may hold values from -3 to 3
- tile_values: bfloat16 [16, 48, 64, 128, 128], P('row', 'col'), may hold values from -0.0625 to 0.0625
- tile_rows: int32 [16, 48, 64], P('row', 'col'), may hold values from 0 to 47
- band_offsets: int32 [16, 48, 64], P('row', 'col'), may hold values from -4 to 4
- tile_count: int32 [16, 48], P('row', 'col'), may hold values from 8 to 64, as said below
- cotangent: bfloat16 [98304, 256], P(('row', 'col')), may hold values from -6 to 6
Outputs:
- activated: bfloat16 [98304, 256], P(('row', 'col'))
- feature_grad: bfloat16 [98304, 128], P(('col', 'row'))
- weight_grad: float32 [128, 256], replicated
- bias_grad: float32 [256], replicated
The draws below stay inside these ranges and needn't reach their ends.
Inputs may be any that keep to these rules, and one draw needn't show every extreme that they name: `tile_count`: the live slots of a device are its first ones; some device has all 64 slots live in every draw.
All inputs are finite; a program needn't handle non-finite values.
Results may differ from the reference program's by a relative error of at most 0.011.
Values may be sent and summed in bfloat16 or wider, within the bound.
No kernel may reach another device: no remote copies, remote signals or barrier semaphores. Data moves between devices by JAX's collectives and lax.ppermute only.
A program may use at most 32 MiB of HBM per device.

```python
import math
import jax
import jax.numpy as jnp
from jax import lax

FIN = 128
HID = 256
NPD = 128
TILE = 128
CAP = 64
BAND = 4
NODES = 98304
RT = 48
CT = 16
N_ROW = 16
N_COL = 48


def draw_tile_count(key, part):
    key = jax.random.fold_in(key, 11)
    subkeys = jax.random.split(key, 4)
    grid_shape = (N_ROW, N_COL)
    light_load = jax.random.randint(subkeys[0], grid_shape, CAP // 8, CAP // 2 + 1)
    heavy_load = jax.random.randint(subkeys[1], grid_shape, CAP // 2, CAP + 1)
    picked = jax.random.randint(subkeys[2], grid_shape, 0, 6) == 0
    slot_counts = jnp.where(picked, heavy_load, light_load).reshape(-1)
    full_spot = jax.random.randint(subkeys[3], (), 0, N_ROW * N_COL)
    slot_counts = slot_counts.at[full_spot].set(CAP)
    return slot_counts.reshape(grid_shape).astype(jnp.int32)


def set_ends(entries, rng, low, largest):
    extent = entries.shape
    place = [jax.random.randint(jax.random.fold_in(rng, axis), (), 0, extent[axis]) for axis in range(len(extent))]
    entries = entries.at[tuple(place)].set(low)
    longest = extent.index(max(extent))
    place[longest] = (place[longest] + 1) % extent[longest]
    return entries.at[tuple(place)].set(largest)


def block_levels(stream_key, shape, cuts, smallest, top_value):
    gain, own = 1.0, jax.random.fold_in(stream_key, 6)
    for position, parts in cuts:
        steps = jnp.exp(jax.random.uniform(jax.random.fold_in(own, position), (parts,), jnp.float32, smallest / len(cuts), top_value / len(cuts)))
        gain = gain * jnp.repeat(steps, shape[position] // parts).reshape([-1 if axis == position else 1 for axis in range(len(shape))])
    return gain


def bell_draw(stream_key, extent, width, bound, pieces=(), kind=jnp.bfloat16):
    values = width * jax.random.normal(stream_key, extent, jnp.float32)
    if pieces:
        values = values * block_levels(stream_key, extent, pieces, -0.22, 0.18)
    return jnp.clip(values, -bound, bound).astype(kind)


def setup_inputs(seed: int = 0) -> dict:
    arg_keys = jax.random.split(jax.random.key(seed), 9)
    return {
        "features": bell_draw(arg_keys[0], (NODES, FIN), 1.0, 6.0, ((0, 768),)),
        "weight": bell_draw(arg_keys[1], (FIN, HID), FIN ** -0.5, 0.5),
        "out_bias": bell_draw(arg_keys[2], (HID,), 0.5, 3.0, (), jnp.float32),
        "tile_values": bell_draw(arg_keys[3], (N_ROW, N_COL, CAP, TILE, TILE), (CAP * TILE * TILE // NPD) ** -0.5, 0.0625, ((0, 16), (1, 48))),
        "tile_rows": set_ends(jax.random.randint(arg_keys[4], (N_ROW, N_COL, CAP), 0, RT), jax.random.fold_in(arg_keys[4], 1), 0, RT - 1).astype(jnp.int32),
        "band_offsets": set_ends(jax.random.randint(arg_keys[5], (N_ROW, N_COL, CAP), 0 - BAND, BAND + 1), jax.random.fold_in(arg_keys[5], 1), 0 - BAND, BAND).astype(jnp.int32),
        "tile_count": draw_tile_count(jax.random.fold_in(arg_keys[8], 71), 0),
        "cotangent": bell_draw(arg_keys[7], (NODES, HID), 1.0, 6.0, ((0, 768),)),
    }


def reference(features, weight, out_bias, tile_values, tile_rows, band_offsets, tile_count, cotangent):
    grid_total = N_ROW * N_COL
    values_flat = tile_values.reshape(grid_total, CAP, TILE, TILE)
    rows_flat = tile_rows.reshape(grid_total, CAP).astype(jnp.int32)
    cols_flat = (rows_flat * CT // RT + band_offsets.reshape(grid_total, CAP)) % CT
    grid_index = jnp.arange(grid_total, dtype=jnp.int32)
    row_global = ((grid_index // N_COL)[:, None] * RT + rows_flat).astype(jnp.int32)
    col_global = ((grid_index % N_COL)[:, None] * CT + cols_flat).astype(jnp.int32)
    slot_index = jnp.arange(CAP, dtype=jnp.int32)[None, :]
    slot_live = (slot_index < tile_count.reshape(grid_total, 1)).astype(jnp.float32)
    feature_tiles = features.reshape(NODES // TILE, TILE, FIN).astype(jnp.float32)

    def forward_turn(running, inputs):
        values_dev, rows_dev, cols_dev, live_dev = inputs
        source = feature_tiles[cols_dev]
        product = jnp.einsum('kij,kjf->kif', values_dev.astype(jnp.float32), source, precision=lax.Precision.HIGHEST)
        return (running.at[rows_dev].add(product * live_dev[:, None, None]), None)
    start_sum = jnp.zeros((NODES // TILE, TILE, FIN), jnp.float32)
    aggregated = lax.scan(forward_turn, start_sum, (values_flat, row_global, col_global, slot_live))[0]
    aggregated = aggregated.reshape(NODES, FIN)
    preact = jnp.dot(aggregated, weight.astype(jnp.float32), precision=lax.Precision.HIGHEST) + out_bias
    sigmoid = jax.nn.sigmoid(preact)
    activated = (preact * sigmoid).astype(jnp.bfloat16)
    grad_pre = (cotangent.astype(jnp.float32) * sigmoid * (1.0 + preact * (1.0 - sigmoid))).astype(jnp.bfloat16)
    grad_float = grad_pre.astype(jnp.float32)
    factor = 1.0 / math.sqrt(NODES)
    weight_grad = jnp.dot(aggregated.T, grad_float, precision=lax.Precision.HIGHEST) * factor
    bias_grad = lax.optimization_barrier(jnp.sum(grad_float, axis=0)) * factor
    projected = jnp.dot(grad_pre, weight.T, preferred_element_type=jnp.float32)
    projected_tiles = projected.reshape(NODES // TILE, TILE, FIN)

    def backward_turn(running, inputs):
        values_dev, rows_dev, cols_dev, live_dev = inputs
        source = projected_tiles[rows_dev]
        product = jnp.einsum('kij,kif->kjf', values_dev.astype(jnp.float32), source, precision=lax.Precision.HIGHEST)
        return (running.at[cols_dev].add(product * live_dev[:, None, None]), None)
    start_back = jnp.zeros((NODES // TILE, TILE, FIN), jnp.float32)
    back_sum = lax.scan(backward_turn, start_back, (values_flat, row_global, col_global, slot_live))[0]
    feature_grad = back_sum.reshape(NODES, FIN).astype(jnp.bfloat16)
    return (activated, feature_grad, weight_grad, bias_grad)
```

```python
import functools
import math

import jax
import jax.numpy as jnp
from jax import lax
from jax.experimental import pallas as pl
from jax.experimental.pallas import tpu as pltpu
from jax.sharding import PartitionSpec as P

TILE = 128
FIN = 128
HID = 256
CAP = 64
RT = 48
CT = 16
STEP = 8
EXTRA = 32
SHARE = 24

SMEM = pl.BlockSpec(memory_space=pltpu.SMEM)
VMEM = pl.BlockSpec(memory_space=pltpu.VMEM)
LIMIT = pltpu.CompilerParams(vmem_limit_bytes=32 * 1024 * 1024)


def dot(a, b, dims=((1,), (0,))):
    return lax.dot_general(a, b, (dims, ((), ())), preferred_element_type=jnp.float32)


def forward_kernel(dst_ref, src_ref, blocks_ref, values_ref, panel_ref, out_ref, acc_ref):
    acc_ref[...] = jnp.zeros_like(acc_ref)

    def step(block, carry):
        for offset in range(STEP):
            k = block * STEP + offset
            product = dot(values_ref[k], panel_ref[src_ref[k]])
            acc_ref[dst_ref[k]] += product
        return carry

    lax.fori_loop(0, blocks_ref[0], step, 0)
    out_ref[...] = acc_ref[:RT].astype(jnp.bfloat16)


def forward(dst, src, blocks, values, panel):
    return pl.pallas_call(
        forward_kernel,
        out_shape=jax.ShapeDtypeStruct((RT, TILE, FIN), jnp.bfloat16),
        in_specs=[SMEM, SMEM, SMEM, VMEM, VMEM],
        out_specs=VMEM,
        scratch_shapes=[pltpu.VMEM((RT + 1, TILE, FIN), jnp.float32)],
        compiler_params=LIMIT,
    )(dst, src, blocks, values, panel)


def local_kernel(parts_ref, cot_ref, weight_ref, bias_ref, act_ref, proj_ref, grads_ref):
    def add(i, total):
        return total + parts_ref[i].astype(jnp.float32)

    agg = lax.fori_loop(1, parts_ref.shape[0], add, parts_ref[0].astype(jnp.float32), unroll=True)
    upper = agg.astype(jnp.bfloat16)
    lower = (agg - upper.astype(jnp.float32)).astype(jnp.bfloat16)
    weight = weight_ref[...]
    preact = dot(upper, weight) + dot(lower, weight) + bias_ref[...]
    sigmoid = 1.0 / (1.0 + jnp.exp(-preact))
    act_ref[...] = (preact * sigmoid).astype(jnp.bfloat16)
    cot = cot_ref[...].astype(jnp.float32)
    grad = (cot * sigmoid * (1.0 + preact * (1.0 - sigmoid))).astype(jnp.bfloat16)
    proj_ref[...] = dot(weight, grad, ((1,), (1,))).astype(jnp.bfloat16)
    over_nodes = ((0,), (0,))
    wgrad = dot(upper, grad, over_nodes) + dot(lower, grad, over_nodes)
    bgrad = jnp.sum(grad.astype(jnp.float32), axis=0, keepdims=True)
    rows = FIN // 8
    for j in range(8):
        grads_ref[j, :rows, :] = wgrad[j * rows : (j + 1) * rows, :FIN]
        grads_ref[8 + j, :rows, :] = wgrad[j * rows : (j + 1) * rows, FIN:]
    tail = jnp.concatenate(
        [bgrad[:, :FIN], bgrad[:, FIN:], jnp.zeros((SHARE - rows - 2, FIN), jnp.float32)], axis=0
    )
    for j in range(16):
        grads_ref[j, rows:, :] = tail


def local_part(parts, cot, weight, bias):
    return pl.pallas_call(
        local_kernel,
        out_shape=(
            jax.ShapeDtypeStruct((TILE, HID), jnp.bfloat16),
            jax.ShapeDtypeStruct((FIN, TILE), jnp.bfloat16),
            jax.ShapeDtypeStruct((CT, SHARE, FIN), jnp.float32),
        ),
        in_specs=[VMEM] * 4,
        out_specs=(VMEM, VMEM, VMEM),
        compiler_params=LIMIT,
    )(parts, cot, weight, bias)


def backward_kernel(dst_ref, src_ref, blocks_ref, values_ref, panel_ref, out_ref, acc_ref):
    acc_ref[...] = jnp.zeros_like(acc_ref)

    def step(block, carry):
        for offset in range(STEP):
            k = block * STEP + offset
            product = dot(panel_ref[src_ref[k], :TILE, :], values_ref[k])
            acc_ref[dst_ref[k]] += product
        return carry

    lax.fori_loop(0, blocks_ref[0], step, 0)
    out_ref[:, :TILE, :] = acc_ref[:CT].astype(jnp.bfloat16)
    share = panel_ref[0, TILE:, :].astype(jnp.float32)
    for i in range(1, panel_ref.shape[0]):
        share = share + panel_ref[i, TILE:, :].astype(jnp.float32)
    share = share.astype(jnp.bfloat16)
    for j in range(CT):
        out_ref[j, TILE:, :] = share


def backward(dst, src, blocks, values, panel):
    return pl.pallas_call(
        backward_kernel,
        out_shape=jax.ShapeDtypeStruct((CT, TILE + EXTRA, TILE), jnp.bfloat16),
        in_specs=[SMEM, SMEM, SMEM, VMEM, VMEM],
        out_specs=VMEM,
        scratch_shapes=[pltpu.VMEM((CT + 1, TILE, TILE), jnp.float32)],
        compiler_params=LIMIT,
    )(dst, src, blocks, values, panel)


def final_kernel(factor, parts_ref, feature_ref, wgrad_ref, bgrad_ref):
    total = parts_ref[0, :TILE, :].astype(jnp.float32)
    for i in range(1, CT):
        total = total + parts_ref[i, :TILE, :].astype(jnp.float32)
    feature_ref[...] = total.T.astype(jnp.bfloat16)
    rows = FIN // 8
    for j in range(8):
        left = parts_ref[j, TILE : TILE + rows, :].astype(jnp.float32) * factor
        right = parts_ref[8 + j, TILE : TILE + rows, :].astype(jnp.float32) * factor
        wgrad_ref[j * rows : (j + 1) * rows, :FIN] = left
        wgrad_ref[j * rows : (j + 1) * rows, FIN:] = right
    tail = parts_ref[0, TILE + rows :, :].astype(jnp.float32) * factor
    bgrad_ref[:, :FIN] = tail[0:1]
    bgrad_ref[:, FIN:] = tail[1:2]


def final_part(parts, factor):
    return pl.pallas_call(
        functools.partial(final_kernel, factor),
        out_shape=(
            jax.ShapeDtypeStruct((TILE, FIN), jnp.bfloat16),
            jax.ShapeDtypeStruct((FIN, HID), jnp.float32),
            jax.ShapeDtypeStruct((1, HID), jnp.float32),
        ),
        in_specs=[VMEM],
        out_specs=(VMEM, VMEM, VMEM),
        compiler_params=LIMIT,
    )(parts)


def local(features, weight, out_bias, tile_values, tile_rows, band_offsets, tile_count, cotangent):
    values = tile_values[0, 0]
    rows = tile_rows[0, 0]
    cols = (rows * CT // RT + band_offsets[0, 0]) % CT
    live = jnp.arange(CAP, dtype=jnp.int32) < tile_count[0, 0]
    blocks = (tile_count[0] + STEP - 1) // STEP
    panel = lax.all_to_all(
        jnp.broadcast_to(features, (CT, TILE, FIN)), "row", 0, 0, tiled=True
    )
    partial = forward(jnp.where(live, rows, RT), cols, blocks, values, panel)
    parts = lax.all_to_all(partial, "col", 0, 0, tiled=True)
    activated, proj, grads = local_part(parts, cotangent, weight, out_bias.reshape(1, HID))
    grads = lax.all_to_all(grads, "row", 0, 0, tiled=True)
    share = jnp.sum(grads, axis=0).astype(jnp.bfloat16)
    block = jnp.concatenate([proj, share, jnp.zeros((EXTRA - SHARE, FIN), jnp.bfloat16)], axis=0)
    targets = lax.all_to_all(
        jnp.broadcast_to(block, (RT, TILE + EXTRA, TILE)), "col", 0, 0, tiled=True
    )
    back = backward(jnp.where(live, cols, CT), rows, blocks, values, targets)
    back = lax.all_to_all(back, "row", 0, 0, tiled=True)
    nodes = TILE * lax.axis_size("row") * lax.axis_size("col")
    feature_grad, weight_grad, bias_grad = final_part(back, 1.0 / math.sqrt(nodes))
    return (activated, feature_grad, weight_grad, bias_grad.reshape(HID))


def solution(mesh):
    placed = (
        P(("col", "row"), None),
        P(),
        P(),
        P("row", "col", None, None, None),
        P("row", "col", None),
        P("row", "col", None),
        P("row", "col"),
        P(("row", "col"), None),
    )
    return jax.shard_map(
        local,
        mesh=mesh,
        in_specs=placed,
        out_specs=(P(("row", "col"), None), P(("col", "row"), None), P(), P()),
        check_vma=False,
    )
```

```python
import functools
import math

import jax
import jax.numpy as jnp
from jax import lax
from jax.experimental import pallas as pl
from jax.experimental.pallas import tpu as pltpu
from jax.sharding import Mesh
from jax.sharding import PartitionSpec as P

TILE = 128
FIN = 128
HID = 256
CAP = 64
RT = 48
CT = 16
STEP = 8
EXTRA = 32
SHARE = 24
NEAR = 4
FAR = RT // NEAR
HALF = FAR // 2
DEPTH = 12
STAGES = 5

ROW = ("yl", "x", "core")
COL = ("yh", "za", "zb")
GROUP = ("yh", "za")
LINE = ("za", "zb")

SMEM = pl.BlockSpec(memory_space=pltpu.SMEM)
VMEM = pl.BlockSpec(memory_space=pltpu.VMEM)
LIMIT = pltpu.CompilerParams(vmem_limit_bytes=32 * 1024 * 1024)
def shift(block, steps):
    return lax.ppermute(block, LINE, [(z, (z + steps) % DEPTH) for z in range(DEPTH)])


def dot(a, b, dims=((1,), (0,))):
    return lax.dot_general(a, b, (dims, ((), ())), preferred_element_type=jnp.float32)


def slot_loop(order_ref, begin, end, add):
    def step(block, carry):
        for offset in range(STEP):
            place = begin + block * STEP + offset
            add(order_ref[0, place], order_ref[1, place], order_ref[2, place], place < end)
        return carry

    lax.fori_loop(0, (end - begin + STEP - 1) // STEP, step, 0)


def forward_slots(stage, base, trash, order_ref, ends_ref, values_ref, panel_ref, acc_ref):
    def add(slot, tile, source, live):
        product = dot(values_ref[slot], panel_ref[source])
        acc_ref[jnp.where(live, base + tile, trash)] += product

    slot_loop(order_ref, ends_ref[stage], ends_ref[stage + 1], add)


def outer_kernel(order_ref, ends_ref, values_ref, panel_ref, *refs):
    next_ref, back_ref, up_ref, down_ref, acc_ref = refs
    acc_ref[...] = jnp.zeros_like(acc_ref)
    trash = 3 * FAR
    for stage in range(1, STAGES):
        base = (min(stage, 3) - 1) * FAR
        forward_slots(stage, base, trash, order_ref, ends_ref, values_ref, panel_ref, acc_ref)
    next_ref[...] = acc_ref[:FAR].astype(jnp.bfloat16)
    back_ref[...] = acc_ref[FAR : 2 * FAR].astype(jnp.bfloat16)
    up_ref[...] = acc_ref[2 * FAR : 2 * FAR + HALF].astype(jnp.bfloat16)
    down_ref[...] = acc_ref[2 * FAR + HALF : 3 * FAR].astype(jnp.bfloat16)


def forward_outer(order, ends, values, panel):
    whole = jax.ShapeDtypeStruct((FAR, TILE, FIN), jnp.bfloat16)
    half = jax.ShapeDtypeStruct((HALF, TILE, FIN), jnp.bfloat16)
    return pl.pallas_call(
        outer_kernel,
        out_shape=(whole, whole, half, half),
        in_specs=[SMEM, SMEM, VMEM, VMEM],
        out_specs=(VMEM,) * 4,
        scratch_shapes=[pltpu.VMEM((3 * FAR + 1, TILE, FIN), jnp.float32)],
        compiler_params=LIMIT,
    )(order, ends, values, panel)


def inner_kernel(order_ref, ends_ref, values_ref, panel_ref, acc_ref):
    acc_ref[...] = jnp.zeros_like(acc_ref)
    forward_slots(0, 0, FAR, order_ref, ends_ref, values_ref, panel_ref, acc_ref)


def forward_inner(order, ends, values, panel):
    return pl.pallas_call(
        inner_kernel,
        out_shape=jax.ShapeDtypeStruct((FAR + 1, TILE, FIN), jnp.float32),
        in_specs=[SMEM, SMEM, VMEM, VMEM],
        out_specs=VMEM,
        compiler_params=LIMIT,
    )(order, ends, values, panel)


def local_kernel(parts_ref, cot_ref, weight_ref, bias_ref, act_ref, proj_ref, grads_ref):
    agg = parts_ref[0].astype(jnp.float32)
    for i in range(1, FAR):
        agg = agg + parts_ref[i].astype(jnp.float32)
    upper = agg.astype(jnp.bfloat16)
    lower = (agg - upper.astype(jnp.float32)).astype(jnp.bfloat16)
    weight = weight_ref[...]
    preact = dot(upper, weight) + dot(lower, weight) + bias_ref[...]
    sigmoid = 1.0 / (1.0 + jnp.exp(-preact))
    act_ref[...] = (preact * sigmoid).astype(jnp.bfloat16)
    cot = cot_ref[...].astype(jnp.float32)
    grad = (cot * sigmoid * (1.0 + preact * (1.0 - sigmoid))).astype(jnp.bfloat16)
    proj_ref[...] = dot(weight, grad, ((1,), (1,))).astype(jnp.bfloat16)
    over_nodes = ((0,), (0,))
    wgrad = dot(upper, grad, over_nodes) + dot(lower, grad, over_nodes)
    bgrad = jnp.sum(grad.astype(jnp.float32), axis=0, keepdims=True)
    rows = FIN // 8
    for j in range(8):
        grads_ref[j, :rows, :] = wgrad[j * rows : (j + 1) * rows, :FIN]
        grads_ref[8 + j, :rows, :] = wgrad[j * rows : (j + 1) * rows, FIN:]
    tail = jnp.concatenate(
        [bgrad[:, :FIN], bgrad[:, FIN:], jnp.zeros((SHARE - rows - 2, FIN), jnp.float32)], axis=0
    )
    for j in range(CT):
        grads_ref[j, rows:, :] = tail


def local_part(parts, cot, weight, bias):
    return pl.pallas_call(
        local_kernel,
        out_shape=(
            jax.ShapeDtypeStruct((TILE, HID), jnp.bfloat16),
            jax.ShapeDtypeStruct((FIN, TILE), jnp.bfloat16),
            jax.ShapeDtypeStruct((CT, SHARE, FIN), jnp.float32),
        ),
        in_specs=[VMEM] * 4,
        out_specs=(VMEM, VMEM, VMEM),
        compiler_params=LIMIT,
    )(parts, cot, weight, bias)


def repeat_kernel(features_ref, out_ref):
    features = features_ref[...]
    for i in range(CT):
        out_ref[i] = features


def repeat(features):
    return pl.pallas_call(
        repeat_kernel,
        out_shape=jax.ShapeDtypeStruct((CT, TILE, FIN), jnp.bfloat16),
        in_specs=[VMEM],
        out_specs=VMEM,
        compiler_params=LIMIT,
    )(features)


def spread_kernel(proj_ref, grads_ref, out_ref):
    share = grads_ref[0]
    for i in range(1, CT):
        share = share + grads_ref[i]
    share = jnp.concatenate([share, jnp.zeros((EXTRA - SHARE, FIN), jnp.float32)], axis=0)
    share = share.astype(jnp.bfloat16)
    proj = proj_ref[...]
    for i in range(FAR):
        out_ref[i, :TILE, :] = proj
        out_ref[i, TILE:, :] = share


def spread(proj, grads):
    return pl.pallas_call(
        spread_kernel,
        out_shape=jax.ShapeDtypeStruct((FAR, TILE + EXTRA, TILE), jnp.bfloat16),
        in_specs=[VMEM, VMEM],
        out_specs=VMEM,
        compiler_params=LIMIT,
    )(proj, grads)


def join_kernel(parts_ref, out_ref, up_ref, down_ref):
    share = parts_ref[0, TILE:, :].astype(jnp.float32)
    for i in range(1, FAR):
        share = share + parts_ref[i, TILE:, :].astype(jnp.float32)
    share = share.astype(jnp.bfloat16)
    middle = HALF * TILE
    for i in range(HALF):
        low = parts_ref[i, :TILE, :]
        out_ref[i * TILE : (i + 1) * TILE, :] = low
        up_ref[i * TILE : (i + 1) * TILE, :] = low
        high = parts_ref[HALF + i, :TILE, :]
        begin = EXTRA + i * TILE
        out_ref[middle + begin : middle + begin + TILE, :] = high
        down_ref[begin : begin + TILE, :] = high
    out_ref[middle : middle + EXTRA, :] = share
    up_ref[middle:, :] = share
    down_ref[:EXTRA, :] = share


def join(parts):
    whole = jax.ShapeDtypeStruct((FAR * TILE + EXTRA, TILE), jnp.bfloat16)
    half = jax.ShapeDtypeStruct((HALF * TILE + EXTRA, TILE), jnp.bfloat16)
    return pl.pallas_call(
        join_kernel,
        out_shape=(whole, half, half),
        in_specs=[VMEM],
        out_specs=(VMEM,) * 3,
        compiler_params=LIMIT,
    )(parts)


def backward_slots(stage, order_ref, ends_ref, values_ref, panel_ref, acc_ref):
    def add(slot, tile, source, live):
        if stage == 4:
            begin = jnp.maximum(tile - HALF, 0) * TILE + EXTRA
        elif stage == 3:
            begin = jnp.minimum(tile, HALF - 1) * TILE
        else:
            begin = tile * TILE + jnp.where(tile < HALF, 0, EXTRA)
        begin = pl.multiple_of(begin, EXTRA)
        product = dot(panel_ref[pl.ds(begin, TILE), :], values_ref[slot])
        acc_ref[jnp.where(live, source, CT)] += product

    slot_loop(order_ref, ends_ref[stage], ends_ref[stage + 1], add)


def first_kernel(order_ref, ends_ref, values_ref, panel_ref, acc_ref):
    acc_ref[...] = jnp.zeros_like(acc_ref)
    backward_slots(0, order_ref, ends_ref, values_ref, panel_ref, acc_ref)


def last_kernel(order_ref, ends_ref, index_ref, values_ref, *refs):
    panels, old_ref, out_ref, acc_ref, shares_ref = refs[:STAGES], *refs[STAGES:]
    acc_ref[...] = old_ref[...]
    for stage in range(1, STAGES):
        backward_slots(stage, order_ref, ends_ref, values_ref, panels[stage], acc_ref)
    out_ref[:, :TILE, :] = acc_ref[:CT].astype(jnp.bfloat16)
    middle = HALF * TILE
    for place, stage in enumerate((0, 1, 3, 2)):
        shares_ref[place] = panels[stage][middle : middle + EXTRA, :].astype(jnp.float32)
    share = shares_ref[index_ref[0]]
    for i in range(1, NEAR):
        share = share + shares_ref[index_ref[i]]
    share = share.astype(jnp.bfloat16)
    for j in range(CT):
        out_ref[j, TILE:, :] = share


ACC = jax.ShapeDtypeStruct((CT + 1, TILE, TILE), jnp.float32)


def backward_first(order, ends, values, panel):
    return pl.pallas_call(
        first_kernel,
        out_shape=ACC,
        in_specs=[SMEM, SMEM, VMEM, VMEM],
        out_specs=VMEM,
        compiler_params=LIMIT,
    )(order, ends, values, panel)


def backward_last(order, ends, index, values, panels, old):
    return pl.pallas_call(
        last_kernel,
        out_shape=jax.ShapeDtypeStruct((CT, TILE + EXTRA, TILE), jnp.bfloat16),
        in_specs=[SMEM, SMEM, SMEM, VMEM] + [VMEM] * (STAGES + 1),
        out_specs=VMEM,
        scratch_shapes=[
            pltpu.VMEM((CT + 1, TILE, TILE), jnp.float32),
            pltpu.VMEM((NEAR, EXTRA, TILE), jnp.float32),
        ],
        compiler_params=LIMIT,
    )(order, ends, index, values, *panels, old)


def final_kernel(factor, parts_ref, feature_ref, wgrad_ref, bgrad_ref):
    total = parts_ref[0, :TILE, :].astype(jnp.float32)
    for i in range(1, CT):
        total = total + parts_ref[i, :TILE, :].astype(jnp.float32)
    feature_ref[...] = total.T.astype(jnp.bfloat16)
    rows = FIN // 8
    for j in range(8):
        left = parts_ref[j, TILE : TILE + rows, :].astype(jnp.float32) * factor
        right = parts_ref[8 + j, TILE : TILE + rows, :].astype(jnp.float32) * factor
        wgrad_ref[j * rows : (j + 1) * rows, :FIN] = left
        wgrad_ref[j * rows : (j + 1) * rows, FIN:] = right
    tail = parts_ref[0, TILE + rows :, :].astype(jnp.float32) * factor
    bgrad_ref[:, :FIN] = tail[0:1]
    bgrad_ref[:, FIN:] = tail[1:2]


def final_part(parts, factor):
    return pl.pallas_call(
        functools.partial(final_kernel, factor),
        out_shape=(
            jax.ShapeDtypeStruct((TILE, FIN), jnp.bfloat16),
            jax.ShapeDtypeStruct((FIN, HID), jnp.float32),
            jax.ShapeDtypeStruct((1, HID), jnp.float32),
        ),
        in_specs=[VMEM],
        out_specs=(VMEM, VMEM, VMEM),
        compiler_params=LIMIT,
    )(parts)


def slot_order(rows, cols, count, zone):
    away = jnp.remainder(rows - zone, NEAR)
    split = jnp.where(rows // NEAR < HALF, 3, 4)
    stage = jnp.where(away == 2, split, jnp.where(away == 3, 2, away))
    slots = jnp.arange(CAP, dtype=jnp.int32)
    stage = jnp.where(slots < count, stage, STAGES)
    key = stage * CAP + slots
    rank = jnp.sum((key[None, :] < key[:, None]).astype(jnp.int32), axis=1)
    places = jnp.arange(CAP + STEP, dtype=jnp.int32)
    chosen = (rank[None, :] == places[:, None]).astype(jnp.int32)
    lists = jnp.stack([slots, rows // NEAR, cols])
    order = jnp.sum(chosen[None] * lists[:, None, :], axis=2)
    ends = jnp.sum(
        (stage[None, :] < jnp.arange(STAGES + 1, dtype=jnp.int32)[:, None]).astype(jnp.int32), axis=1
    )
    return order, ends


def local(features, weight, out_bias, tile_values, tile_rows, band_offsets, tile_count, cotangent):
    values = tile_values[0, 0]
    rows = tile_rows[0, 0]
    cols = jnp.remainder(rows * CT // RT + band_offsets[0, 0], CT)
    zone = lax.axis_index("zb")
    order, ends = slot_order(rows, cols, tile_count[0, 0], zone)
    panel = lax.all_to_all(repeat(features), ROW, 0, 0, tiled=True)
    to_next, to_back, to_up, to_down = forward_outer(order, ends, values, panel)
    arrived = (shift(to_next, 1), shift(to_back, -1))
    arrived += (jnp.concatenate([shift(to_up, 2), shift(to_down, -2)], axis=0),)
    summed = forward_inner(order, ends, values, panel)[:FAR]
    for part in arrived:
        summed = summed + part.astype(jnp.float32)
    parts = lax.all_to_all(summed.astype(jnp.bfloat16), GROUP, 0, 0, tiled=True)
    activated, proj, grads = local_part(parts, cotangent, weight, out_bias.reshape(1, HID))
    grads = lax.all_to_all(grads, ROW, 0, 0, tiled=True)
    targets = lax.all_to_all(spread(proj, grads), GROUP, 0, 0, tiled=True)
    panel, up, down = join(targets)
    panels = [panel, shift(panel, -1), shift(panel, 1), shift(up, 2), shift(down, -2)]
    acc = backward_first(order, ends, values, panel)
    index = jnp.remainder(jnp.arange(NEAR, dtype=jnp.int32) - zone, NEAR)
    back = backward_last(order, ends, index, values, panels, acc)
    back = lax.all_to_all(back, ROW, 0, 0, tiled=True)
    nodes = TILE * lax.axis_size(ROW) * lax.axis_size(COL)
    feature_grad, weight_grad, bias_grad = final_part(back, 1.0 / math.sqrt(nodes))
    return (activated, feature_grad, weight_grad, bias_grad.reshape(HID))


def solution(mesh):
    axes = ROW + COL
    fine = Mesh(mesh.devices.reshape(2, 4, 2, 4, DEPTH // NEAR, NEAR), axes)
    placed = (
        P(COL + ROW, None),
        P(),
        P(),
        P(ROW, COL, None, None, None),
        P(ROW, COL, None),
        P(ROW, COL, None),
        P(ROW, COL),
        P(ROW + COL, None),
    )
    return jax.shard_map(
        local,
        mesh=fine,
        in_specs=placed,
        out_specs=(P(ROW + COL, None), P(COL + ROW, None), P(), P()),
        check_vma=False,
    )
```

```python
import functools
import math

import jax
import jax.numpy as jnp
from jax import lax
from jax.experimental import pallas as pl
from jax.experimental.pallas import tpu as pltpu
from jax.sharding import Mesh
from jax.sharding import PartitionSpec as P

TILE = 128
FIN = 128
HID = 256
CAP = 64
RT = 48
CT = 16
STEP = 8
EXTRA = 32
SHARE = 24
PART = FIN * HID // (CT * TILE)
NEAR = 4
FAR = RT // NEAR
HALF = FAR // 2
DEPTH = 12
STAGES = 5

ROW = ("yl", "x", "core")
COL = ("yh", "za", "zb")
GROUP = ("yh", "za")
LINE = ("za", "zb")

SMEM = pl.BlockSpec(memory_space=pltpu.SMEM)
VMEM = pl.BlockSpec(memory_space=pltpu.VMEM)
LIMIT = pltpu.CompilerParams(vmem_limit_bytes=32 * 1024 * 1024)
def shift(block, steps):
    return lax.ppermute(block, LINE, [(z, (z + steps) % DEPTH) for z in range(DEPTH)])


def dot(a, b, dims=((1,), (0,))):
    return lax.dot_general(a, b, (dims, ((), ())), preferred_element_type=jnp.float32)


def slot_loop(order_ref, begin, end, add):
    def step(block, carry):
        for offset in range(STEP):
            place = begin + block * STEP + offset
            add(order_ref[0, place], order_ref[1, place], order_ref[2, place], place < end)
        return carry

    lax.fori_loop(0, (end - begin + STEP - 1) // STEP, step, 0)


def forward_slots(stage, base, trash, order_ref, ends_ref, values_ref, panel_ref, acc_ref):
    def add(slot, tile, source, live):
        product = dot(values_ref[slot], panel_ref[source])
        acc_ref[jnp.where(live, base + tile, trash)] += product

    slot_loop(order_ref, ends_ref[stage], ends_ref[stage + 1], add)


def outer_kernel(order_ref, ends_ref, values_ref, panel_ref, *refs):
    next_ref, back_ref, up_ref, down_ref, acc_ref = refs
    acc_ref[...] = jnp.zeros_like(acc_ref)
    trash = 3 * FAR
    for stage in range(1, STAGES):
        base = (min(stage, 3) - 1) * FAR
        forward_slots(stage, base, trash, order_ref, ends_ref, values_ref, panel_ref, acc_ref)
    next_ref[...] = acc_ref[:FAR].astype(jnp.bfloat16)
    back_ref[...] = acc_ref[FAR : 2 * FAR].astype(jnp.bfloat16)
    up_ref[...] = acc_ref[2 * FAR : 2 * FAR + HALF].astype(jnp.bfloat16)
    down_ref[...] = acc_ref[2 * FAR + HALF : 3 * FAR].astype(jnp.bfloat16)


def forward_outer(order, ends, values, panel):
    whole = jax.ShapeDtypeStruct((FAR, TILE, FIN), jnp.bfloat16)
    half = jax.ShapeDtypeStruct((HALF, TILE, FIN), jnp.bfloat16)
    return pl.pallas_call(
        outer_kernel,
        out_shape=(whole, whole, half, half),
        in_specs=[SMEM, SMEM, VMEM, VMEM],
        out_specs=(VMEM,) * 4,
        scratch_shapes=[pltpu.VMEM((3 * FAR + 1, TILE, FIN), jnp.float32)],
        compiler_params=LIMIT,
    )(order, ends, values, panel)


def inner_kernel(order_ref, ends_ref, values_ref, panel_ref, acc_ref):
    acc_ref[...] = jnp.zeros_like(acc_ref)
    forward_slots(0, 0, FAR, order_ref, ends_ref, values_ref, panel_ref, acc_ref)


def forward_inner(order, ends, values, panel):
    return pl.pallas_call(
        inner_kernel,
        out_shape=jax.ShapeDtypeStruct((FAR + 1, TILE, FIN), jnp.float32),
        in_specs=[SMEM, SMEM, VMEM, VMEM],
        out_specs=VMEM,
        compiler_params=LIMIT,
    )(order, ends, values, panel)


def local_kernel(parts_ref, cot_ref, weight_ref, bias_ref, act_ref, proj_ref, grads_ref):
    agg = parts_ref[0].astype(jnp.float32)
    for i in range(1, FAR):
        agg = agg + parts_ref[i].astype(jnp.float32)
    upper = agg.astype(jnp.bfloat16)
    lower = (agg - upper.astype(jnp.float32)).astype(jnp.bfloat16)
    weight = weight_ref[...]
    preact = dot(upper, weight) + dot(lower, weight) + bias_ref[...]
    sigmoid = 1.0 / (1.0 + jnp.exp(-preact))
    act_ref[...] = (preact * sigmoid).astype(jnp.bfloat16)
    cot = cot_ref[...].astype(jnp.float32)
    grad = (cot * sigmoid * (1.0 + preact * (1.0 - sigmoid))).astype(jnp.bfloat16)
    proj_ref[...] = dot(weight, grad, ((1,), (1,))).astype(jnp.bfloat16)
    over_nodes = ((0,), (0,))
    wgrad = dot(upper, grad, over_nodes) + dot(lower, grad, over_nodes)
    bgrad = jnp.sum(grad.astype(jnp.float32), axis=0, keepdims=True)
    rows = FIN // 8
    for j in range(8):
        grads_ref[j, :rows, :] = wgrad[j * rows : (j + 1) * rows, :FIN]
        grads_ref[8 + j, :rows, :] = wgrad[j * rows : (j + 1) * rows, FIN:]
    tail = jnp.concatenate(
        [bgrad[:, :FIN], bgrad[:, FIN:], jnp.zeros((SHARE - rows - 2, FIN), jnp.float32)], axis=0
    )
    for j in range(CT):
        grads_ref[j, rows:, :] = tail


def local_part(parts, cot, weight, bias):
    return pl.pallas_call(
        local_kernel,
        out_shape=(
            jax.ShapeDtypeStruct((TILE, HID), jnp.bfloat16),
            jax.ShapeDtypeStruct((FIN, TILE), jnp.bfloat16),
            jax.ShapeDtypeStruct((CT, SHARE, FIN), jnp.float32),
        ),
        in_specs=[VMEM] * 4,
        out_specs=(VMEM, VMEM, VMEM),
        compiler_params=LIMIT,
    )(parts, cot, weight, bias)


def repeat_kernel(features_ref, out_ref):
    features = features_ref[...]
    for i in range(CT):
        out_ref[i] = features


def repeat(features):
    return pl.pallas_call(
        repeat_kernel,
        out_shape=jax.ShapeDtypeStruct((CT, TILE, FIN), jnp.bfloat16),
        in_specs=[VMEM],
        out_specs=VMEM,
        compiler_params=LIMIT,
    )(features)


def fetch_kernel(values_ref, out_ref, sems):
    part = CAP // STEP
    copies = []
    for i in range(STEP):
        rows = pl.ds(i * part, part)
        copies.append(pltpu.make_async_copy(values_ref.at[rows], out_ref.at[rows], sems.at[i]))
    for copy in copies:
        copy.start()
    for copy in copies:
        copy.wait()


def fetch(values):
    return pl.pallas_call(
        fetch_kernel,
        out_shape=jax.ShapeDtypeStruct(values.shape, values.dtype),
        in_specs=[pl.BlockSpec(memory_space=pl.ANY)],
        out_specs=VMEM,
        scratch_shapes=[pltpu.SemaphoreType.DMA((STEP,))],
        compiler_params=LIMIT,
        cost_estimate=pl.CostEstimate(flops=0, bytes_accessed=1 << 22, transcendentals=0),
    )(values)


def spread_kernel(proj_ref, grads_ref, out_ref):
    share = grads_ref[0]
    for i in range(1, CT):
        share = share + grads_ref[i]
    share = jnp.concatenate([share, jnp.zeros((EXTRA - SHARE, FIN), jnp.float32)], axis=0)
    share = share.astype(jnp.bfloat16)
    proj = proj_ref[...]
    for i in range(FAR):
        out_ref[i, :TILE, :] = proj
        out_ref[i, TILE:, :] = share


def spread(proj, grads):
    return pl.pallas_call(
        spread_kernel,
        out_shape=jax.ShapeDtypeStruct((FAR, TILE + EXTRA, TILE), jnp.bfloat16),
        in_specs=[VMEM, VMEM],
        out_specs=VMEM,
        compiler_params=LIMIT,
    )(proj, grads)


def join_kernel(parts_ref, out_ref, up_ref, down_ref):
    share = parts_ref[0, TILE:, :].astype(jnp.float32)
    for i in range(1, FAR):
        share = share + parts_ref[i, TILE:, :].astype(jnp.float32)
    share = share.astype(jnp.bfloat16)
    middle = HALF * TILE
    for i in range(HALF):
        low = parts_ref[i, :TILE, :]
        out_ref[i * TILE : (i + 1) * TILE, :] = low
        up_ref[i * TILE : (i + 1) * TILE, :] = low
        high = parts_ref[HALF + i, :TILE, :]
        begin = EXTRA + i * TILE
        out_ref[middle + begin : middle + begin + TILE, :] = high
        down_ref[begin : begin + TILE, :] = high
    out_ref[middle : middle + EXTRA, :] = share
    up_ref[middle:, :] = share
    down_ref[:EXTRA, :] = share


def join(parts):
    whole = jax.ShapeDtypeStruct((FAR * TILE + EXTRA, TILE), jnp.bfloat16)
    half = jax.ShapeDtypeStruct((HALF * TILE + EXTRA, TILE), jnp.bfloat16)
    return pl.pallas_call(
        join_kernel,
        out_shape=(whole, half, half),
        in_specs=[VMEM],
        out_specs=(VMEM,) * 3,
        compiler_params=LIMIT,
    )(parts)


def backward_slots(stage, order_ref, ends_ref, values_ref, panel_ref, acc_ref):
    def add(slot, tile, source, live):
        if stage == 4:
            begin = jnp.maximum(tile - HALF, 0) * TILE + EXTRA
        elif stage == 3:
            begin = jnp.minimum(tile, HALF - 1) * TILE
        else:
            begin = tile * TILE + jnp.where(tile < HALF, 0, EXTRA)
        begin = pl.multiple_of(begin, EXTRA)
        product = dot(panel_ref[pl.ds(begin, TILE), :], values_ref[slot])
        acc_ref[jnp.where(live, source, CT)] += product

    slot_loop(order_ref, ends_ref[stage], ends_ref[stage + 1], add)


def first_kernel(order_ref, ends_ref, values_ref, panel_ref, acc_ref):
    acc_ref[...] = jnp.zeros_like(acc_ref)
    backward_slots(0, order_ref, ends_ref, values_ref, panel_ref, acc_ref)


def last_kernel(factor, order_ref, ends_ref, index_ref, values_ref, *refs):
    panels, old_ref, out_ref, bgrad_ref, acc_ref, shares_ref = refs[:STAGES], *refs[STAGES:]
    acc_ref[...] = old_ref[...]
    for stage in range(1, STAGES):
        backward_slots(stage, order_ref, ends_ref, values_ref, panels[stage], acc_ref)
    out_ref[:, :TILE, :] = acc_ref[:CT].astype(jnp.bfloat16)
    middle = HALF * TILE
    for place, stage in enumerate((0, 1, 3, 2)):
        shares_ref[place] = panels[stage][middle : middle + EXTRA, :].astype(jnp.float32)
    share = shares_ref[index_ref[0]]
    for i in range(1, NEAR):
        share = share + shares_ref[index_ref[i]]
    bgrad_ref[:, :FIN] = share[PART : PART + 1] * factor
    bgrad_ref[:, FIN:] = share[PART + 1 : PART + 2] * factor
    share = share[:PART].astype(jnp.bfloat16)
    for j in range(CT):
        out_ref[j, TILE:, :] = share


ACC = jax.ShapeDtypeStruct((CT + 1, TILE, TILE), jnp.float32)


def backward_first(order, ends, values, panel):
    return pl.pallas_call(
        first_kernel,
        out_shape=ACC,
        in_specs=[SMEM, SMEM, VMEM, VMEM],
        out_specs=VMEM,
        compiler_params=LIMIT,
    )(order, ends, values, panel)


def backward_last(factor, order, ends, index, values, panels, old):
    return pl.pallas_call(
        functools.partial(last_kernel, factor),
        out_shape=(
            jax.ShapeDtypeStruct((CT, TILE + PART, TILE), jnp.bfloat16),
            jax.ShapeDtypeStruct((1, HID), jnp.float32),
        ),
        in_specs=[SMEM, SMEM, SMEM, VMEM] + [VMEM] * (STAGES + 1),
        out_specs=(VMEM, VMEM),
        scratch_shapes=[
            pltpu.VMEM((CT + 1, TILE, TILE), jnp.float32),
            pltpu.VMEM((NEAR, EXTRA, TILE), jnp.float32),
        ],
        compiler_params=LIMIT,
    )(order, ends, index, values, *panels, old)


def final_kernel(factor, parts_ref, feature_ref, wgrad_ref):
    total = parts_ref[0, :TILE, :].astype(jnp.float32)
    for i in range(1, CT):
        total = total + parts_ref[i, :TILE, :].astype(jnp.float32)
    feature_ref[...] = total.T.astype(jnp.bfloat16)
    half = CT // 2
    for j in range(half):
        left = parts_ref[j, TILE:, :].astype(jnp.float32) * factor
        right = parts_ref[half + j, TILE:, :].astype(jnp.float32) * factor
        wgrad_ref[j * PART : (j + 1) * PART, :FIN] = left
        wgrad_ref[j * PART : (j + 1) * PART, FIN:] = right


def final_part(parts, factor):
    return pl.pallas_call(
        functools.partial(final_kernel, factor),
        out_shape=(
            jax.ShapeDtypeStruct((TILE, FIN), jnp.bfloat16),
            jax.ShapeDtypeStruct((FIN, HID), jnp.float32),
        ),
        in_specs=[VMEM],
        out_specs=(VMEM, VMEM),
        compiler_params=LIMIT,
    )(parts)


def slot_order(rows, cols, count, zone):
    away = jnp.remainder(rows - zone, NEAR)
    split = jnp.where(rows // NEAR < HALF, 3, 4)
    stage = jnp.where(away == 2, split, jnp.where(away == 3, 2, away))
    slots = jnp.arange(CAP, dtype=jnp.int32)
    stage = jnp.where(slots < count, stage, STAGES)
    key = stage * CAP + slots
    rank = jnp.sum((key[None, :] < key[:, None]).astype(jnp.int32), axis=1)
    places = jnp.arange(CAP + STEP, dtype=jnp.int32)
    chosen = (rank[None, :] == places[:, None]).astype(jnp.int32)
    lists = jnp.stack([slots, rows // NEAR, cols])
    order = jnp.sum(chosen[None] * lists[:, None, :], axis=2)
    ends = jnp.sum(
        (stage[None, :] < jnp.arange(STAGES + 1, dtype=jnp.int32)[:, None]).astype(jnp.int32), axis=1
    )
    return order, ends


def local(features, weight, out_bias, tile_values, tile_rows, band_offsets, tile_count, cotangent):
    values = fetch(tile_values[0, 0])
    rows = tile_rows[0, 0]
    cols = jnp.remainder(rows * CT // RT + band_offsets[0, 0], CT)
    zone = lax.axis_index("zb")
    order, ends = slot_order(rows, cols, tile_count[0, 0], zone)
    panel = lax.all_to_all(repeat(features), ROW, 0, 0, tiled=True)
    to_next, to_back, to_up, to_down = forward_outer(order, ends, values, panel)
    arrived = (shift(to_next, 1), shift(to_back, -1))
    arrived += (jnp.concatenate([shift(to_up, 2), shift(to_down, -2)], axis=0),)
    summed = forward_inner(order, ends, values, panel)[:FAR]
    for part in arrived:
        summed = summed + part.astype(jnp.float32)
    parts = lax.all_to_all(summed.astype(jnp.bfloat16), GROUP, 0, 0, tiled=True)
    activated, proj, grads = local_part(parts, cotangent, weight, out_bias.reshape(1, HID))
    grads = lax.all_to_all(grads, ROW, 0, 0, tiled=True)
    targets = lax.all_to_all(spread(proj, grads), GROUP, 0, 0, tiled=True)
    panel, up, down = join(targets)
    panels = [panel, shift(panel, -1), shift(panel, 1), shift(up, 2), shift(down, -2)]
    acc = backward_first(order, ends, values, panel)
    index = jnp.remainder(jnp.arange(NEAR, dtype=jnp.int32) - zone, NEAR)
    factor = 1.0 / math.sqrt(TILE * lax.axis_size(ROW) * lax.axis_size(COL))
    back, bias_grad = backward_last(factor, order, ends, index, values, panels, acc)
    back = lax.all_to_all(back, ROW, 0, 0, tiled=True)
    feature_grad, weight_grad = final_part(back, factor)
    return (activated, feature_grad, weight_grad, bias_grad.reshape(HID))


def solution(mesh):
    axes = ROW + COL
    fine = Mesh(mesh.devices.reshape(2, 4, 2, 4, DEPTH // NEAR, NEAR), axes)
    placed = (
        P(COL + ROW, None),
        P(),
        P(),
        P(ROW, COL, None, None, None),
        P(ROW, COL, None),
        P(ROW, COL, None),
        P(ROW, COL),
        P(ROW + COL, None),
    )
    return jax.shard_map(
        local,
        mesh=fine,
        in_specs=placed,
        out_specs=(P(ROW + COL, None), P(COL + ROW, None), P(), P()),
        check_vma=False,
    )
```

```python
import functools
import math

import jax
import jax.numpy as jnp
from jax import lax
from jax.experimental import pallas as pl
from jax.experimental.pallas import tpu as pltpu
from jax.sharding import Mesh
from jax.sharding import PartitionSpec as P

TILE = 128
FIN = 128
HID = 256
CAP = 64
RT = 48
CT = 16
STEP = 8
EXTRA = 32
SHARE = 24
PART = FIN * HID // (CT * TILE)
NEAR = 3
FAR = RT // NEAR
DEPTH = 12
STAGES = NEAR

ROW = ("yl", "x", "core")
COL = ("yh", "za", "zb")
TALL = 4
WIDE = FAR // TALL
LINE = ("za", "zb")

SMEM = pl.BlockSpec(memory_space=pltpu.SMEM)
VMEM = pl.BlockSpec(memory_space=pltpu.VMEM)
LIMIT = pltpu.CompilerParams(vmem_limit_bytes=32 * 1024 * 1024)
def shift(block, steps):
    return lax.ppermute(block, LINE, [(z, (z + steps) % DEPTH) for z in range(DEPTH)])


def dot(a, b, dims=((1,), (0,))):
    return lax.dot_general(a, b, (dims, ((), ())), preferred_element_type=jnp.float32)


def slot_loop(order_ref, begin, end, add):
    def step(block, carry):
        for offset in range(STEP):
            place = begin + block * STEP + offset
            add(order_ref[0, place], order_ref[1, place], order_ref[2, place], place < end)
        return carry

    lax.fori_loop(0, (end - begin + STEP - 1) // STEP, step, 0)


def forward_slots(stage, base, trash, order_ref, ends_ref, values_ref, panel_ref, acc_ref):
    def add(slot, tile, source, live):
        product = dot(values_ref[slot], panel_ref[source])
        acc_ref[jnp.where(live, base + tile, trash)] += product

    slot_loop(order_ref, ends_ref[stage], ends_ref[stage + 1], add)


def outer_kernel(order_ref, ends_ref, values_ref, panel_ref, *refs):
    outs, acc_ref = refs[:-1], refs[-1]
    acc_ref[...] = jnp.zeros_like(acc_ref)
    trash = (NEAR - 1) * FAR
    for stage in range(1, NEAR):
        base = (stage - 1) * FAR
        forward_slots(stage, base, trash, order_ref, ends_ref, values_ref, panel_ref, acc_ref)
        outs[stage - 1][...] = acc_ref[base : base + FAR].astype(jnp.bfloat16)


def forward_outer(order, ends, values, panel):
    sent = jax.ShapeDtypeStruct((FAR, TILE, FIN), jnp.bfloat16)
    return pl.pallas_call(
        outer_kernel,
        out_shape=(sent,) * (NEAR - 1),
        in_specs=[SMEM, SMEM, VMEM, VMEM],
        out_specs=(VMEM,) * (NEAR - 1),
        scratch_shapes=[pltpu.VMEM(((NEAR - 1) * FAR + 1, TILE, FIN), jnp.float32)],
        compiler_params=LIMIT,
    )(order, ends, values, panel)


def inner_kernel(order_ref, ends_ref, values_ref, panel_ref, acc_ref):
    acc_ref[...] = jnp.zeros_like(acc_ref)
    forward_slots(0, 0, FAR, order_ref, ends_ref, values_ref, panel_ref, acc_ref)


def forward_inner(order, ends, values, panel):
    return pl.pallas_call(
        inner_kernel,
        out_shape=jax.ShapeDtypeStruct((FAR + 1, TILE, FIN), jnp.float32),
        in_specs=[SMEM, SMEM, VMEM, VMEM],
        out_specs=VMEM,
        compiler_params=LIMIT,
    )(order, ends, values, panel)


def local_kernel(parts_ref, cot_ref, weight_ref, bias_ref, act_ref, proj_ref, grads_ref):
    agg = parts_ref[0].astype(jnp.float32)
    for i in range(1, FAR):
        agg = agg + parts_ref[i].astype(jnp.float32)
    upper = agg.astype(jnp.bfloat16)
    lower = (agg - upper.astype(jnp.float32)).astype(jnp.bfloat16)
    weight = weight_ref[...]
    preact = dot(upper, weight) + dot(lower, weight) + bias_ref[...]
    sigmoid = 1.0 / (1.0 + jnp.exp(-preact))
    act_ref[...] = (preact * sigmoid).astype(jnp.bfloat16)
    cot = cot_ref[...].astype(jnp.float32)
    grad = (cot * sigmoid * (1.0 + preact * (1.0 - sigmoid))).astype(jnp.bfloat16)
    proj_ref[...] = dot(weight, grad, ((1,), (1,))).astype(jnp.bfloat16)
    over_nodes = ((0,), (0,))
    wgrad = dot(upper, grad, over_nodes) + dot(lower, grad, over_nodes)
    bgrad = jnp.sum(grad.astype(jnp.float32), axis=0, keepdims=True)
    rows = FIN // 8
    for j in range(8):
        grads_ref[j, :rows, :] = wgrad[j * rows : (j + 1) * rows, :FIN]
        grads_ref[8 + j, :rows, :] = wgrad[j * rows : (j + 1) * rows, FIN:]
    tail = jnp.concatenate(
        [bgrad[:, :FIN], bgrad[:, FIN:], jnp.zeros((SHARE - rows - 2, FIN), jnp.float32)], axis=0
    )
    for j in range(CT):
        grads_ref[j, rows:, :] = tail


def local_part(parts, cot, weight, bias):
    return pl.pallas_call(
        local_kernel,
        out_shape=(
            jax.ShapeDtypeStruct((TILE, HID), jnp.bfloat16),
            jax.ShapeDtypeStruct((FIN, TILE), jnp.bfloat16),
            jax.ShapeDtypeStruct((CT, SHARE, FIN), jnp.float32),
        ),
        in_specs=[VMEM] * 4,
        out_specs=(VMEM, VMEM, VMEM),
        compiler_params=LIMIT,
    )(parts, cot, weight, bias)


def repeat_kernel(features_ref, out_ref):
    features = features_ref[...]
    for i in range(CT):
        out_ref[i] = features


def repeat(features):
    return pl.pallas_call(
        repeat_kernel,
        out_shape=jax.ShapeDtypeStruct((CT, TILE, FIN), jnp.bfloat16),
        in_specs=[VMEM],
        out_specs=VMEM,
        compiler_params=LIMIT,
    )(features)


def fetch_kernel(values_ref, out_ref, sems):
    part = CAP // STEP
    copies = []
    for i in range(STEP):
        rows = pl.ds(i * part, part)
        copies.append(pltpu.make_async_copy(values_ref.at[rows], out_ref.at[rows], sems.at[i]))
    for copy in copies:
        copy.start()
    for copy in copies:
        copy.wait()


def fetch(values):
    return pl.pallas_call(
        fetch_kernel,
        out_shape=jax.ShapeDtypeStruct(values.shape, values.dtype),
        in_specs=[pl.BlockSpec(memory_space=pl.ANY)],
        out_specs=VMEM,
        scratch_shapes=[pltpu.SemaphoreType.DMA((STEP,))],
        compiler_params=LIMIT,
        cost_estimate=pl.CostEstimate(flops=0, bytes_accessed=1 << 22, transcendentals=0),
    )(values)


def spread_kernel(proj_ref, grads_ref, out_ref):
    share = grads_ref[0]
    for i in range(1, CT):
        share = share + grads_ref[i]
    share = jnp.concatenate([share, jnp.zeros((EXTRA - SHARE, FIN), jnp.float32)], axis=0)
    share = share.astype(jnp.bfloat16)
    proj = proj_ref[...]
    for i in range(WIDE):
        out_ref[i, :TILE, :] = proj
        out_ref[i, TILE:, :] = share


def spread(proj, grads):
    return pl.pallas_call(
        spread_kernel,
        out_shape=jax.ShapeDtypeStruct((WIDE, TILE + EXTRA, TILE), jnp.bfloat16),
        in_specs=[VMEM, VMEM],
        out_specs=VMEM,
        compiler_params=LIMIT,
    )(proj, grads)


def widen_kernel(parts_ref, out_ref):
    share = parts_ref[0, TILE:, :].astype(jnp.float32)
    for i in range(1, WIDE):
        share = share + parts_ref[i, TILE:, :].astype(jnp.float32)
    share = share.astype(jnp.bfloat16)
    for i in range(WIDE):
        tile = parts_ref[i, :TILE, :]
        for j in range(TALL):
            out_ref[j, i * TILE : (i + 1) * TILE, :] = tile
    for j in range(TALL):
        out_ref[j, WIDE * TILE :, :] = share


def widen(parts):
    return pl.pallas_call(
        widen_kernel,
        out_shape=jax.ShapeDtypeStruct((TALL, WIDE * TILE + EXTRA, TILE), jnp.bfloat16),
        in_specs=[VMEM],
        out_specs=VMEM,
        compiler_params=LIMIT,
    )(parts)


def join_kernel(parts_ref, out_ref):
    last = WIDE * TILE
    share = parts_ref[0, last:, :].astype(jnp.float32)
    for i in range(1, TALL):
        share = share + parts_ref[i, last:, :].astype(jnp.float32)
    for i in range(TALL):
        out_ref[i * last : (i + 1) * last, :] = parts_ref[i, :last, :]
    out_ref[FAR * TILE :, :] = share.astype(jnp.bfloat16)


def join(parts):
    return pl.pallas_call(
        join_kernel,
        out_shape=jax.ShapeDtypeStruct((FAR * TILE + EXTRA, TILE), jnp.bfloat16),
        in_specs=[VMEM],
        out_specs=VMEM,
        compiler_params=LIMIT,
    )(parts)


def backward_slots(stage, order_ref, ends_ref, values_ref, panel_ref, acc_ref):
    def add(slot, tile, source, live):
        begin = pl.multiple_of(tile * TILE, TILE)
        product = dot(panel_ref[pl.ds(begin, TILE), :], values_ref[slot])
        acc_ref[jnp.where(live, source, CT)] += product

    slot_loop(order_ref, ends_ref[stage], ends_ref[stage + 1], add)


def first_kernel(order_ref, ends_ref, values_ref, panel_ref, acc_ref):
    acc_ref[...] = jnp.zeros_like(acc_ref)
    backward_slots(0, order_ref, ends_ref, values_ref, panel_ref, acc_ref)


def last_kernel(factor, order_ref, ends_ref, index_ref, values_ref, *refs):
    panels, old_ref, out_ref, bgrad_ref, acc_ref, shares_ref = refs[:STAGES], *refs[STAGES:]
    acc_ref[...] = old_ref[...]
    for stage in range(1, STAGES):
        backward_slots(stage, order_ref, ends_ref, values_ref, panels[stage], acc_ref)
    out_ref[:, :TILE, :] = acc_ref[:CT].astype(jnp.bfloat16)
    for stage in range(NEAR):
        shares_ref[stage] = panels[stage][FAR * TILE :, :].astype(jnp.float32)
    share = shares_ref[index_ref[0]]
    for i in range(1, NEAR):
        share = share + shares_ref[index_ref[i]]
    bgrad_ref[:, :FIN] = share[PART : PART + 1] * factor
    bgrad_ref[:, FIN:] = share[PART + 1 : PART + 2] * factor
    share = share[:PART].astype(jnp.bfloat16)
    for j in range(CT):
        out_ref[j, TILE:, :] = share


ACC = jax.ShapeDtypeStruct((CT + 1, TILE, TILE), jnp.float32)


def backward_first(order, ends, values, panel):
    return pl.pallas_call(
        first_kernel,
        out_shape=ACC,
        in_specs=[SMEM, SMEM, VMEM, VMEM],
        out_specs=VMEM,
        compiler_params=LIMIT,
    )(order, ends, values, panel)


def backward_last(factor, order, ends, index, values, panels, old):
    return pl.pallas_call(
        functools.partial(last_kernel, factor),
        out_shape=(
            jax.ShapeDtypeStruct((CT, TILE + PART, TILE), jnp.bfloat16),
            jax.ShapeDtypeStruct((1, HID), jnp.float32),
        ),
        in_specs=[SMEM, SMEM, SMEM, VMEM] + [VMEM] * (STAGES + 1),
        out_specs=(VMEM, VMEM),
        scratch_shapes=[
            pltpu.VMEM((CT + 1, TILE, TILE), jnp.float32),
            pltpu.VMEM((NEAR, EXTRA, TILE), jnp.float32),
        ],
        compiler_params=LIMIT,
    )(order, ends, index, values, *panels, old)


def final_kernel(factor, parts_ref, feature_ref, wgrad_ref):
    total = parts_ref[0, :TILE, :].astype(jnp.float32)
    for i in range(1, CT):
        total = total + parts_ref[i, :TILE, :].astype(jnp.float32)
    feature_ref[...] = total.T.astype(jnp.bfloat16)
    half = CT // 2
    for j in range(half):
        left = parts_ref[j, TILE:, :].astype(jnp.float32) * factor
        right = parts_ref[half + j, TILE:, :].astype(jnp.float32) * factor
        wgrad_ref[j * PART : (j + 1) * PART, :FIN] = left
        wgrad_ref[j * PART : (j + 1) * PART, FIN:] = right


def final_part(parts, factor):
    return pl.pallas_call(
        functools.partial(final_kernel, factor),
        out_shape=(
            jax.ShapeDtypeStruct((TILE, FIN), jnp.bfloat16),
            jax.ShapeDtypeStruct((FIN, HID), jnp.float32),
        ),
        in_specs=[VMEM],
        out_specs=(VMEM, VMEM),
        compiler_params=LIMIT,
    )(parts)


def slot_order(rows, cols, count, zone):
    stage = jnp.remainder(rows - zone, NEAR)
    slots = jnp.arange(CAP, dtype=jnp.int32)
    stage = jnp.where(slots < count, stage, STAGES)
    key = stage * CAP + slots
    rank = jnp.sum((key[None, :] < key[:, None]).astype(jnp.int32), axis=1)
    places = jnp.arange(CAP + STEP, dtype=jnp.int32)
    chosen = (rank[None, :] == places[:, None]).astype(jnp.int32)
    lists = jnp.stack([slots, rows // NEAR, cols])
    order = jnp.sum(chosen[None] * lists[:, None, :], axis=2)
    ends = jnp.sum(
        (stage[None, :] < jnp.arange(STAGES + 1, dtype=jnp.int32)[:, None]).astype(jnp.int32), axis=1
    )
    return order, ends


def local(features, weight, out_bias, tile_values, tile_rows, band_offsets, tile_count, cotangent):
    values = fetch(tile_values[0, 0])
    rows = tile_rows[0, 0]
    cols = jnp.remainder(rows * CT // RT + band_offsets[0, 0], CT)
    zone = lax.axis_index("zb")
    order, ends = slot_order(rows, cols, tile_count[0, 0], zone)
    panel = lax.all_to_all(repeat(features), ROW, 0, 0, tiled=True)
    to_next, to_back = forward_outer(order, ends, values, panel)
    arrived = (shift(to_next, 1), shift(to_back, -1))
    summed = forward_inner(order, ends, values, panel)[:FAR]
    for part in arrived:
        summed = summed + part.astype(jnp.float32)
    parts = lax.all_to_all(summed.astype(jnp.bfloat16), ("yh", "za"), 0, 0, tiled=True)
    activated, proj, grads = local_part(parts, cotangent, weight, out_bias.reshape(1, HID))
    grads = lax.all_to_all(grads, ROW, 0, 0, tiled=True)
    targets = lax.all_to_all(spread(proj, grads), "za", 0, 0, tiled=True)
    targets = lax.all_to_all(widen(targets), "yh", 0, 0, tiled=True)
    panel = join(targets)
    panels = [panel, shift(panel, -1), shift(panel, 1)]
    acc = backward_first(order, ends, values, panel)
    index = jnp.remainder(jnp.arange(NEAR, dtype=jnp.int32) - zone, NEAR)
    factor = 1.0 / math.sqrt(TILE * lax.axis_size(ROW) * lax.axis_size(COL))
    back, bias_grad = backward_last(factor, order, ends, index, values, panels, acc)
    back = lax.all_to_all(back, ROW, 0, 0, tiled=True)
    feature_grad, weight_grad = final_part(back, factor)
    return (activated, feature_grad, weight_grad, bias_grad.reshape(HID))


def solution(mesh):
    axes = ROW + COL
    fine = Mesh(mesh.devices.reshape(2, 4, 2, 4, DEPTH // NEAR, NEAR), axes)
    placed = (
        P(COL + ROW, None),
        P(),
        P(),
        P(ROW, COL, None, None, None),
        P(ROW, COL, None),
        P(ROW, COL, None),
        P(ROW, COL),
        P(ROW + COL, None),
    )
    return jax.shard_map(
        local,
        mesh=fine,
        in_specs=placed,
        out_specs=(P(ROW + COL, None), P(COL + ROW, None), P(), P()),
        check_vma=False,
    )
```

```python
import functools
import math

import jax
import jax.numpy as jnp
from jax import lax
from jax.experimental import pallas as pl
from jax.experimental.pallas import tpu as pltpu
from jax.sharding import Mesh
from jax.sharding import PartitionSpec as P

TILE = 128
FIN = 128
HID = 256
CAP = 64
RT = 48
CT = 16
STEP = 8
EXTRA = 32
SHARE = 24
PART = FIN * HID // (CT * TILE)
NEAR = 4
FAR = RT // NEAR
HALF = FAR // 2
DEPTH = 12
STAGES = 5

ROW = ("yl", "x", "core")
COL = ("yh", "za", "zb")
GROUP = ("yh", "za")
LINE = ("za", "zb")

SMEM = pl.BlockSpec(memory_space=pltpu.SMEM)
VMEM = pl.BlockSpec(memory_space=pltpu.VMEM)
LIMIT = pltpu.CompilerParams(vmem_limit_bytes=32 * 1024 * 1024)
def shift(block, steps):
    return lax.ppermute(block, LINE, [(z, (z + steps) % DEPTH) for z in range(DEPTH)])


def dot(a, b, dims=((1,), (0,))):
    return lax.dot_general(a, b, (dims, ((), ())), preferred_element_type=jnp.float32)


def slot_loop(order_ref, begin, end, add):
    def step(block, carry):
        for offset in range(STEP):
            place = begin + block * STEP + offset
            add(order_ref[0, place], order_ref[1, place], order_ref[2, place], place < end)
        return carry

    lax.fori_loop(0, (end - begin + STEP - 1) // STEP, step, 0)


def forward_slots(stage, base, trash, order_ref, ends_ref, values_ref, panel_ref, acc_ref):
    def add(slot, tile, source, live):
        product = dot(values_ref[slot], panel_ref[source])
        acc_ref[jnp.where(live, base + tile, trash)] += product

    slot_loop(order_ref, ends_ref[stage], ends_ref[stage + 1], add)


def near_kernel(order_ref, ends_ref, values_ref, panel_ref, next_ref, back_ref, acc_ref):
    acc_ref[...] = jnp.zeros_like(acc_ref)
    for stage in (1, 2):
        base = (stage - 1) * FAR
        forward_slots(stage, base, 2 * FAR, order_ref, ends_ref, values_ref, panel_ref, acc_ref)
    next_ref[...] = acc_ref[:FAR].astype(jnp.bfloat16)
    back_ref[...] = acc_ref[FAR : 2 * FAR].astype(jnp.bfloat16)


def rest_kernel(order_ref, ends_ref, values_ref, panel_ref, up_ref, down_ref, own_ref, acc_ref):
    own_ref[...] = jnp.zeros_like(own_ref)
    acc_ref[...] = jnp.zeros_like(acc_ref)
    for stage in (3, 4):
        forward_slots(stage, 0, FAR, order_ref, ends_ref, values_ref, panel_ref, acc_ref)
    up_ref[...] = acc_ref[:HALF].astype(jnp.bfloat16)
    down_ref[...] = acc_ref[HALF:FAR].astype(jnp.bfloat16)
    forward_slots(0, 0, FAR, order_ref, ends_ref, values_ref, panel_ref, own_ref)


def forward(kernel, shapes, tiles, order, ends, values, panel):
    return pl.pallas_call(
        kernel,
        out_shape=shapes,
        in_specs=[SMEM, SMEM, VMEM, VMEM],
        out_specs=(VMEM,) * len(shapes),
        scratch_shapes=[pltpu.VMEM((tiles + 1, TILE, FIN), jnp.float32)],
        compiler_params=LIMIT,
    )(order, ends, values, panel)


def local_kernel(parts_ref, cot_ref, weight_ref, bias_ref, act_ref, proj_ref, grads_ref):
    agg = parts_ref[0].astype(jnp.float32)
    for i in range(1, FAR):
        agg = agg + parts_ref[i].astype(jnp.float32)
    upper = agg.astype(jnp.bfloat16)
    lower = (agg - upper.astype(jnp.float32)).astype(jnp.bfloat16)
    weight = weight_ref[...]
    preact = dot(upper, weight) + dot(lower, weight) + bias_ref[...]
    sigmoid = 1.0 / (1.0 + jnp.exp(-preact))
    act_ref[...] = (preact * sigmoid).astype(jnp.bfloat16)
    cot = cot_ref[...].astype(jnp.float32)
    grad = (cot * sigmoid * (1.0 + preact * (1.0 - sigmoid))).astype(jnp.bfloat16)
    proj_ref[...] = dot(weight, grad, ((1,), (1,))).astype(jnp.bfloat16)
    over_nodes = ((0,), (0,))
    wgrad = dot(upper, grad, over_nodes) + dot(lower, grad, over_nodes)
    bgrad = jnp.sum(grad.astype(jnp.float32), axis=0, keepdims=True)
    rows = FIN // 8
    for j in range(8):
        grads_ref[j, :rows, :] = wgrad[j * rows : (j + 1) * rows, :FIN]
        grads_ref[8 + j, :rows, :] = wgrad[j * rows : (j + 1) * rows, FIN:]
    tail = jnp.concatenate(
        [bgrad[:, :FIN], bgrad[:, FIN:], jnp.zeros((SHARE - rows - 2, FIN), jnp.float32)], axis=0
    )
    for j in range(CT):
        grads_ref[j, rows:, :] = tail


def local_part(parts, cot, weight, bias):
    return pl.pallas_call(
        local_kernel,
        out_shape=(
            jax.ShapeDtypeStruct((TILE, HID), jnp.bfloat16),
            jax.ShapeDtypeStruct((FIN, TILE), jnp.bfloat16),
            jax.ShapeDtypeStruct((CT, SHARE, FIN), jnp.float32),
        ),
        in_specs=[VMEM] * 4,
        out_specs=(VMEM, VMEM, VMEM),
        compiler_params=LIMIT,
    )(parts, cot, weight, bias)


def repeat_kernel(features_ref, out_ref):
    features = features_ref[...]
    for i in range(CT):
        out_ref[i] = features


def repeat(features):
    return pl.pallas_call(
        repeat_kernel,
        out_shape=jax.ShapeDtypeStruct((CT, TILE, FIN), jnp.bfloat16),
        in_specs=[VMEM],
        out_specs=VMEM,
        compiler_params=LIMIT,
    )(features)


def fetch_kernel(values_ref, out_ref, sems):
    part = CAP // STEP
    copies = []
    for i in range(STEP):
        rows = pl.ds(i * part, part)
        copies.append(pltpu.make_async_copy(values_ref.at[rows], out_ref.at[rows], sems.at[i]))
    for copy in copies:
        copy.start()
    for copy in copies:
        copy.wait()


def fetch(values):
    return pl.pallas_call(
        fetch_kernel,
        out_shape=jax.ShapeDtypeStruct(values.shape, values.dtype),
        in_specs=[pl.BlockSpec(memory_space=pl.ANY)],
        out_specs=VMEM,
        scratch_shapes=[pltpu.SemaphoreType.DMA((STEP,))],
        compiler_params=LIMIT,
        cost_estimate=pl.CostEstimate(flops=0, bytes_accessed=1 << 22, transcendentals=0),
    )(values)


def spread_kernel(proj_ref, grads_ref, out_ref):
    share = grads_ref[0]
    for i in range(1, CT):
        share = share + grads_ref[i]
    share = jnp.concatenate([share, jnp.zeros((EXTRA - SHARE, FIN), jnp.float32)], axis=0)
    share = share.astype(jnp.bfloat16)
    proj = proj_ref[...]
    for i in range(FAR):
        out_ref[i, :TILE, :] = proj
        out_ref[i, TILE:, :] = share


def spread(proj, grads):
    return pl.pallas_call(
        spread_kernel,
        out_shape=jax.ShapeDtypeStruct((FAR, TILE + EXTRA, TILE), jnp.bfloat16),
        in_specs=[VMEM, VMEM],
        out_specs=VMEM,
        compiler_params=LIMIT,
    )(proj, grads)


def join_kernel(parts_ref, out_ref, up_ref, down_ref):
    share = parts_ref[0, TILE:, :].astype(jnp.float32)
    for i in range(1, FAR):
        share = share + parts_ref[i, TILE:, :].astype(jnp.float32)
    share = share.astype(jnp.bfloat16)
    middle = HALF * TILE
    for i in range(HALF):
        low = parts_ref[i, :TILE, :]
        out_ref[i * TILE : (i + 1) * TILE, :] = low
        up_ref[i * TILE : (i + 1) * TILE, :] = low
        high = parts_ref[HALF + i, :TILE, :]
        begin = EXTRA + i * TILE
        out_ref[middle + begin : middle + begin + TILE, :] = high
        down_ref[begin : begin + TILE, :] = high
    out_ref[middle : middle + EXTRA, :] = share
    up_ref[middle:, :] = share
    down_ref[:EXTRA, :] = share


def join(parts):
    whole = jax.ShapeDtypeStruct((FAR * TILE + EXTRA, TILE), jnp.bfloat16)
    half = jax.ShapeDtypeStruct((HALF * TILE + EXTRA, TILE), jnp.bfloat16)
    return pl.pallas_call(
        join_kernel,
        out_shape=(whole, half, half),
        in_specs=[VMEM],
        out_specs=(VMEM,) * 3,
        compiler_params=LIMIT,
    )(parts)


def backward_slots(stage, order_ref, ends_ref, values_ref, panel_ref, acc_ref):
    def add(slot, tile, source, live):
        if stage == 4:
            begin = jnp.maximum(tile - HALF, 0) * TILE + EXTRA
        elif stage == 3:
            begin = jnp.minimum(tile, HALF - 1) * TILE
        else:
            begin = tile * TILE + jnp.where(tile < HALF, 0, EXTRA)
        begin = pl.multiple_of(begin, EXTRA)
        product = dot(panel_ref[pl.ds(begin, TILE), :], values_ref[slot])
        acc_ref[jnp.where(live, source, CT)] += product

    slot_loop(order_ref, ends_ref[stage], ends_ref[stage + 1], add)


def first_kernel(order_ref, ends_ref, values_ref, panel_ref, acc_ref):
    acc_ref[...] = jnp.zeros_like(acc_ref)
    backward_slots(0, order_ref, ends_ref, values_ref, panel_ref, acc_ref)


def middle_kernel(order_ref, ends_ref, values_ref, next_ref, back_ref, old_ref, acc_ref):
    acc_ref[...] = old_ref[...]
    backward_slots(1, order_ref, ends_ref, values_ref, next_ref, acc_ref)
    backward_slots(2, order_ref, ends_ref, values_ref, back_ref, acc_ref)


def last_kernel(factor, order_ref, ends_ref, index_ref, values_ref, *refs):
    panels, old_ref, out_ref, bgrad_ref, acc_ref, shares_ref = refs[:STAGES], *refs[STAGES:]
    acc_ref[...] = old_ref[...]
    for stage in (3, 4):
        backward_slots(stage, order_ref, ends_ref, values_ref, panels[stage], acc_ref)
    out_ref[:, :TILE, :] = acc_ref[:CT].astype(jnp.bfloat16)
    middle = HALF * TILE
    for place, stage in enumerate((0, 1, 3, 2)):
        shares_ref[place] = panels[stage][middle : middle + EXTRA, :].astype(jnp.float32)
    share = shares_ref[index_ref[0]]
    for i in range(1, NEAR):
        share = share + shares_ref[index_ref[i]]
    bgrad_ref[:, :FIN] = share[PART : PART + 1] * factor
    bgrad_ref[:, FIN:] = share[PART + 1 : PART + 2] * factor
    share = share[:PART].astype(jnp.bfloat16)
    for j in range(CT):
        out_ref[j, TILE:, :] = share


ACC = jax.ShapeDtypeStruct((CT + 1, TILE, TILE), jnp.float32)


def backward_first(order, ends, values, panel):
    return pl.pallas_call(
        first_kernel,
        out_shape=ACC,
        in_specs=[SMEM, SMEM, VMEM, VMEM],
        out_specs=VMEM,
        compiler_params=LIMIT,
    )(order, ends, values, panel)


def backward_middle(order, ends, values, panels, old):
    return pl.pallas_call(
        middle_kernel,
        out_shape=ACC,
        in_specs=[SMEM, SMEM] + [VMEM] * 4,
        out_specs=VMEM,
        compiler_params=LIMIT,
    )(order, ends, values, *panels, old)


def backward_last(factor, order, ends, index, values, panels, old):
    return pl.pallas_call(
        functools.partial(last_kernel, factor),
        out_shape=(
            jax.ShapeDtypeStruct((CT, TILE + PART, TILE), jnp.bfloat16),
            jax.ShapeDtypeStruct((1, HID), jnp.float32),
        ),
        in_specs=[SMEM, SMEM, SMEM, VMEM] + [VMEM] * (STAGES + 1),
        out_specs=(VMEM, VMEM),
        scratch_shapes=[
            pltpu.VMEM((CT + 1, TILE, TILE), jnp.float32),
            pltpu.VMEM((NEAR, EXTRA, TILE), jnp.float32),
        ],
        compiler_params=LIMIT,
    )(order, ends, index, values, *panels, old)


def final_kernel(factor, parts_ref, feature_ref, wgrad_ref):
    total = parts_ref[0, :TILE, :].astype(jnp.float32)
    for i in range(1, CT):
        total = total + parts_ref[i, :TILE, :].astype(jnp.float32)
    feature_ref[...] = total.T.astype(jnp.bfloat16)
    half = CT // 2
    for j in range(half):
        left = parts_ref[j, TILE:, :].astype(jnp.float32) * factor
        right = parts_ref[half + j, TILE:, :].astype(jnp.float32) * factor
        wgrad_ref[j * PART : (j + 1) * PART, :FIN] = left
        wgrad_ref[j * PART : (j + 1) * PART, FIN:] = right


def final_part(parts, factor):
    return pl.pallas_call(
        functools.partial(final_kernel, factor),
        out_shape=(
            jax.ShapeDtypeStruct((TILE, FIN), jnp.bfloat16),
            jax.ShapeDtypeStruct((FIN, HID), jnp.float32),
        ),
        in_specs=[VMEM],
        out_specs=(VMEM, VMEM),
        compiler_params=LIMIT,
    )(parts)


def slot_order(rows, cols, count, zone):
    away = jnp.remainder(rows - zone, NEAR)
    split = jnp.where(rows // NEAR < HALF, 3, 4)
    stage = jnp.where(away == 2, split, jnp.where(away == 3, 2, away))
    slots = jnp.arange(CAP, dtype=jnp.int32)
    stage = jnp.where(slots < count, stage, STAGES)
    key = stage * CAP + slots
    rank = jnp.sum((key[None, :] < key[:, None]).astype(jnp.int32), axis=1)
    places = jnp.arange(CAP + STEP, dtype=jnp.int32)
    chosen = (rank[None, :] == places[:, None]).astype(jnp.int32)
    lists = jnp.stack([slots, rows // NEAR, cols])
    order = jnp.sum(chosen[None] * lists[:, None, :], axis=2)
    ends = jnp.sum(
        (stage[None, :] < jnp.arange(STAGES + 1, dtype=jnp.int32)[:, None]).astype(jnp.int32), axis=1
    )
    return order, ends


def local(features, weight, out_bias, tile_values, tile_rows, band_offsets, tile_count, cotangent):
    values = fetch(tile_values[0, 0])
    rows = tile_rows[0, 0]
    cols = jnp.remainder(rows * CT // RT + band_offsets[0, 0], CT)
    zone = lax.axis_index("zb")
    order, ends = slot_order(rows, cols, tile_count[0, 0], zone)
    panel = lax.all_to_all(repeat(features), ROW, 0, 0, tiled=True)
    whole = jax.ShapeDtypeStruct((FAR, TILE, FIN), jnp.bfloat16)
    half = jax.ShapeDtypeStruct((HALF, TILE, FIN), jnp.bfloat16)
    own = jax.ShapeDtypeStruct((FAR + 1, TILE, FIN), jnp.float32)
    slots = (order, ends, values, panel)
    to_next, to_back = forward(near_kernel, (whole, whole), 2 * FAR, *slots)
    arrived = (shift(to_next, 1), shift(to_back, -1))
    to_up, to_down, own = forward(rest_kernel, (half, half, own), FAR, *slots)
    arrived += (jnp.concatenate([shift(to_up, 2), shift(to_down, -2)], axis=0),)
    summed = own[:FAR]
    for part in arrived:
        summed = summed + part.astype(jnp.float32)
    parts = lax.all_to_all(summed.astype(jnp.bfloat16), GROUP, 0, 0, tiled=True)
    activated, proj, grads = local_part(parts, cotangent, weight, out_bias.reshape(1, HID))
    grads = lax.all_to_all(grads, ROW, 0, 0, tiled=True)
    targets = lax.all_to_all(spread(proj, grads), GROUP, 0, 0, tiled=True)
    panel, up, down = join(targets)
    panels = [panel, shift(panel, -1), shift(panel, 1), shift(up, 2), shift(down, -2)]
    acc = backward_first(order, ends, values, panel)
    acc = backward_middle(order, ends, values, panels[1:3], acc)
    index = jnp.remainder(jnp.arange(NEAR, dtype=jnp.int32) - zone, NEAR)
    factor = 1.0 / math.sqrt(TILE * lax.axis_size(ROW) * lax.axis_size(COL))
    back, bias_grad = backward_last(factor, order, ends, index, values, panels, acc)
    back = lax.all_to_all(back, ROW, 0, 0, tiled=True)
    feature_grad, weight_grad = final_part(back, factor)
    return (activated, feature_grad, weight_grad, bias_grad.reshape(HID))


def solution(mesh):
    axes = ROW + COL
    fine = Mesh(mesh.devices.reshape(2, 4, 2, 4, DEPTH // NEAR, NEAR), axes)
    placed = (
        P(COL + ROW, None),
        P(),
        P(),
        P(ROW, COL, None, None, None),
        P(ROW, COL, None),
        P(ROW, COL, None),
        P(ROW, COL),
        P(ROW + COL, None),
    )
    return jax.shard_map(
        local,
        mesh=fine,
        in_specs=placed,
        out_specs=(P(ROW + COL, None), P(COL + ROW, None), P(), P()),
        check_vma=False,
    )
```
